32 devices in a mesh: seq: 4 (over y, core), mem: 8 (over z, x).
Axes of the slice: x: 2, y: 2, z: 4, core: 2. Of those that a mesh axis runs over, the one named last changes fastest.
Arguments:
- queries: bfloat16 [128, 64, 2048], P('mem', 'seq'), may hold values from -40 to 40
- keys: bfloat16 [32, 128, 2048], P('mem'), may hold values from -8 to 8
- values: bfloat16 [32, 128, 2048], P('mem'), may hold values from -6 to 6
- grad_out: bfloat16 [128, 64, 2048], P('mem', 'seq'), may hold values from -6 to 6
- neighbour_owner: int32 [128, 2], replicated, may hold values from 0 to 7, all different within a row; in each aligned block of 16 rows (0 to 15, 16 to 31, ...) at most 6 rows name the same one
- neighbour_row: int32 [128, 2], replicated, may hold values from 0 to 3
Outputs:
- attended: bfloat16 [128, 64, 2048], P('mem', 'seq')
- grad_queries: bfloat16 [128, 64, 2048], P('mem', 'seq')
- grad_keys: bfloat16 [32, 128, 2048], P('mem', 'seq')
- grad_values: bfloat16 [32, 128, 2048], P('mem', 'seq')
The draws below stay inside these ranges and needn't reach their ends.
Inputs may be any that keep to these rules, and one draw needn't show every extreme that they name: `neighbour_owner`: A group's two entries lie on different shards. Among the 16 groups of one index of mem (aligned blocks of rows) at most 6 name one shard, and exactly 6 do for some shard.
All inputs are finite; a program needn't handle non-finite values.
Results may differ from the reference program's by a relative error of at most 0.015.
Values may be sent and summed in bfloat16 or wider, within the bound.
A program may use at most 128 MiB of HBM per device.

```python
import math
import jax
import jax.numpy as jnp
import numpy as np
from jax import lax

HEADS = 16
HEAD_DIM = 128
GROUP_LEN = 64
NEIGH_LEN = 128
GROUP_DEV = 16
NEIGH_SHARD = 4
GROUPS = 128
NEIGHBOURS = 32
CAP = 6
N_MEM = 8


def draw_queries(key, part):
    shape = (GROUPS, GROUP_LEN, HEADS * HEAD_DIM)
    inner = jax.random.fold_in(key, 11)
    base = jax.random.normal(inner, shape, jnp.float32)
    return jnp.clip(base, -6.0, 6.0).astype(jnp.bfloat16)


def draw_keys(key, part):
    shape = (NEIGHBOURS, NEIGH_LEN, HEADS * HEAD_DIM)
    inner = jax.random.fold_in(key, 13)
    base = jax.random.normal(inner, shape, jnp.float32)
    return jnp.clip(base, -6.0, 6.0).astype(jnp.bfloat16)


def plant(values, rng, least, top_value):
    index_at = [jax.random.randint(jax.random.fold_in(rng, axis), (), 0, length) for axis, length in enumerate(values.shape)]
    widest = values.shape.index(max(values.shape))
    neighbour = index_at[:widest] + [(index_at[widest] + 1) % values.shape[widest]] + index_at[widest + 1:]
    return values.at[tuple(index_at)].set(least).at[tuple(neighbour)].set(top_value)


def steps_of(rng, extent, cuts, least, top_value):
    factor_of = 1.0
    for axis_at, shards_of in cuts:
        steps = jax.random.uniform(jax.random.fold_in(jax.random.fold_in(rng, 6), axis_at), (shards_of,), jnp.float32, least / len(cuts), top_value / len(cuts))
        factor_of = factor_of * jnp.repeat(jnp.exp(steps), extent[axis_at] // shards_of).reshape((-1,) + (1,) * (len(extent) - 1 - axis_at))
    return factor_of


def assign_block(rng, own, number, rows, count, top, bound, lean):
    order = jax.random.permutation(rng, count)
    heavy_load, ordinary = shares(count, rows * top, bound, lean, True), shares(count, rows * top, bound, lean, False)
    places = jnp.arange(count)

    def named(lengths, turn):
        used = int((lengths > 0).sum())
        fixed = max(1, used // 4)
        moved = fixed + (places - fixed + turn * (used - fixed)) % max(1, count - fixed)
        return jnp.zeros((count,), jnp.int32).at[order[jnp.where(places < fixed, places, moved)]].set(jnp.asarray(lengths, jnp.int32))

    lengths = jnp.where(number % 4 == 0, named(heavy_load, number // 4), named(ordinary, number - number // 4 - 1))
    mixed = jax.random.permutation(jax.random.fold_in(own, 3), count)
    donor, sink = mixed[0:count // 2 * 2:2], mixed[1:count // 2 * 2:2]
    room = jnp.minimum(lengths[donor] - 1, bound - lengths[sink]) // 2
    room = jnp.where((donor == order[0]) | (sink == order[0]) | (lengths[sink] == 0), 0, jnp.maximum(room, 0))
    moved = jax.random.randint(jax.random.fold_in(own, 4), (count // 2,), 0, 1 << 20) % (room + 1)
    lengths = lengths.at[donor].add(-moved).at[sink].add(moved)
    items = jnp.searchsorted(jnp.cumsum(lengths), jnp.arange(rows * top), side="right").astype(jnp.int32)
    table = items.reshape(top, rows).T
    table = table[jax.random.permutation(jax.random.fold_in(own, 1), rows)]
    turn = jax.random.randint(jax.random.fold_in(own, 2), (rows, 1), 0, top)
    return jnp.take_along_axis(table, (jnp.arange(top)[None, :] + turn) % top, axis=1)


def shares(count, total, most, slope, full):
    loads = [(1 << 20) // math.isqrt(grade ** slope) + 1 for grade in range(1, count + 1)]
    largest = most if full else min(most, max(-(-total // count), total * loads[0] // sum(loads)))
    least = 1 if total - largest >= count - 1 else 0
    holding, surplus = [largest] + [least] * (count - 1), total - largest - least * (count - 1)
    while surplus > 0:
        candidates = [i for i in range(1, count) if holding[i] < largest] or [i for i in range(1, count) if holding[i] < most]
        whole, remaining = sum([loads[i] for i in candidates]), surplus
        for i in candidates:
            extra = min(most - holding[i], max(1, remaining * loads[i] // whole), surplus)
            holding[i] = holding[i] + extra
            surplus = surplus - extra
    return np.array(holding)


def noise(rng, dims, width, reach, shards=(), dtype=jnp.bfloat16):
    level = steps_of(rng, dims, shards, -0.22, 0.18) if shards else 1.0
    drawn = jax.random.normal(rng, dims, jnp.float32) * width * level
    return jnp.minimum(jnp.maximum(drawn, -reach), reach).astype(dtype)


def setup_inputs(seed: int = 0) -> dict:
    key_of = jax.random.split(jax.random.key(seed), 7)
    queries = draw_queries(jax.random.fold_in(key_of[6], 71), 0)
    keys = draw_keys(jax.random.fold_in(key_of[6], 71), 0)
    values = noise(key_of[2], (NEIGHBOURS, NEIGH_LEN, HEADS * HEAD_DIM), 1.0, 6.0, ((0, 8),))
    grad_out = noise(key_of[3], (GROUPS, GROUP_LEN, HEADS * HEAD_DIM), 1.0, 6.0, ((0, 8), (1, 4)))
    neighbour_owner_keys = jax.random.split(jax.random.fold_in(key_of[4], 1), GROUPS // GROUP_DEV)
    neighbour_owner_turns = jax.random.permutation(jax.random.fold_in(key_of[4], 3), GROUPS // GROUP_DEV)
    neighbour_owner = jax.vmap(lambda own, number: assign_block(jax.random.fold_in(key_of[4], 2), own, number, GROUP_DEV, N_MEM, 2, CAP, 2))(neighbour_owner_keys, neighbour_owner_turns).reshape((GROUPS, 2))
    neighbour_row = plant(jax.random.randint(key_of[5], (GROUPS, 2), 0, NEIGH_SHARD), jax.random.fold_in(key_of[5], 1), 0, NEIGH_SHARD - 1).astype(jnp.int32)
    return {"queries": queries, "keys": keys, "values": values, "grad_out": grad_out, "neighbour_owner": neighbour_owner, "neighbour_row": neighbour_row}


def half_round(array):
    return lax.optimization_barrier(array.astype(jnp.bfloat16)).astype(jnp.float32)

def reference(queries, keys, values, grad_out, neighbour_owner, neighbour_row):
    scaling = 1.0 / math.sqrt(HEAD_DIM)
    feature_count = HEADS * HEAD_DIM
    neighbour_ids = (neighbour_owner * NEIGH_SHARD + neighbour_row).astype(jnp.int32)
    keys_heads = keys.reshape(NEIGHBOURS, NEIGH_LEN, HEADS, HEAD_DIM)
    values_heads = values.reshape(NEIGHBOURS, NEIGH_LEN, HEADS, HEAD_DIM)

    def block_step(carried, inputs):
        key_acc, value_acc = carried
        query_block, cotangent, ids_block = inputs
        query_f = query_block.reshape(GROUP_DEV, GROUP_LEN, HEADS, HEAD_DIM).astype(jnp.float32)
        grad_f = cotangent.reshape(GROUP_DEV, GROUP_LEN, HEADS, HEAD_DIM).astype(jnp.float32)
        key_f = keys_heads[ids_block].astype(jnp.float32)
        value_f = values_heads[ids_block].astype(jnp.float32)
        scores = jnp.einsum('bthd,bjkhd->bjthk', query_f, key_f) * scaling
        own_peak = lax.optimization_barrier(jnp.max(scores, axis=4))
        exponent = half_round(jnp.exp(scores - own_peak[..., None]))
        own_norm = lax.optimization_barrier(jnp.sum(exponent, axis=4))
        partial_mix = jnp.einsum('bjthk,bjkhd->bjthd', exponent, value_f) / own_norm[..., None]
        row_top = lax.optimization_barrier(jnp.max(own_peak, axis=1))
        weight = jnp.exp(own_peak - row_top[:, None]) * own_norm
        row_norm = lax.optimization_barrier(jnp.sum(weight, axis=1))
        attended = (lax.optimization_barrier(jnp.sum(weight[..., None] * partial_mix, axis=1)) / row_norm[..., None]).astype(jnp.bfloat16)
        attended_f = attended.astype(jnp.float32)
        row_dsum = lax.optimization_barrier(jnp.sum(grad_f * attended_f, axis=3))
        probability = jnp.exp(scores - row_top[:, None, :, :, None]) / row_norm[:, None, :, :, None]
        prob_half = half_round(probability)
        value_grad = jnp.einsum('bjthk,bthd->bjkhd', prob_half, grad_f)
        prob_grad = jnp.einsum('bthd,bjkhd->bjthk', grad_f, value_f)
        score_half = half_round(probability * (prob_grad - row_dsum[:, None, :, :, None]) * scaling)
        query_parts = jnp.einsum('bjthk,bjkhd->bjthd', score_half, key_f)
        query_grad = query_parts[:, 0] + query_parts[:, 1]
        key_grad = jnp.einsum('bjthk,bthd->bjkhd', score_half, query_f)
        flat_ids = ids_block.reshape(-1)
        key_acc = key_acc.at[flat_ids].add(key_grad.reshape(2 * GROUP_DEV, NEIGH_LEN, feature_count))
        value_acc = value_acc.at[flat_ids].add(value_grad.reshape(2 * GROUP_DEV, NEIGH_LEN, feature_count))
        outputs = (attended.reshape(GROUP_DEV, GROUP_LEN, feature_count), query_grad.astype(jnp.bfloat16).reshape(GROUP_DEV, GROUP_LEN, feature_count))
        return ((key_acc, value_acc), outputs)
    start = (jnp.zeros((NEIGHBOURS, NEIGH_LEN, feature_count), jnp.float32), jnp.zeros((NEIGHBOURS, NEIGH_LEN, feature_count), jnp.float32))
    inputs = (queries.reshape(N_MEM, GROUP_DEV, GROUP_LEN, feature_count), grad_out.reshape(N_MEM, GROUP_DEV, GROUP_LEN, feature_count), neighbour_ids.reshape(N_MEM, GROUP_DEV, 2))
    (key_total, value_total), (attended_all, query_all) = lax.scan(block_step, start, inputs)
    attended_out = attended_all.reshape(GROUPS, GROUP_LEN, feature_count)
    query_out = query_all.reshape(GROUPS, GROUP_LEN, feature_count)
    return (attended_out, query_out, key_total.astype(jnp.bfloat16), value_total.astype(jnp.bfloat16))
```

```python
import functools
import math

import jax
import jax.numpy as jnp
from jax import lax
from jax.experimental import pallas as pl
from jax.experimental.pallas import tpu as pltpu
from jax.sharding import PartitionSpec as P

HEADS = 16
UNROLL = 4


def matmul(a, b, contract):
    return lax.dot_general(a, b, (contract, ((), ())), preferred_element_type=jnp.float32)


def attention_kernel(scaling, nbr, tokens, memory, outs, grads, sums):
    groups = tokens.shape[1]
    key_len = memory.shape[2]
    sums[...] = jnp.zeros_like(sums)

    def one_group(c, _):
        first, second = nbr[c, 0], nbr[c, 1]
        query, grad = tokens[0, c], tokens[1, c]
        key = jnp.concatenate([memory[first, 0], memory[second, 0]], axis=0)
        value = jnp.concatenate([memory[first, 1], memory[second, 1]], axis=0)
        scores = matmul(query, key, ((1,), (1,))) * scaling
        prob_grad = matmul(grad, value, ((1,), (1,)))
        top = jnp.max(scores, axis=1, keepdims=True)
        exponent = jnp.exp(scores - top)
        norm = jnp.sum(exponent, axis=1, keepdims=True)
        prob = exponent / norm
        prob_half = prob.astype(jnp.bfloat16)
        attended = matmul(prob_half, value, ((1,), (0,))).astype(jnp.bfloat16)
        dsum = jnp.sum(
            grad.astype(jnp.float32) * attended.astype(jnp.float32), axis=1, keepdims=True
        )
        score_half = (prob * (prob_grad - dsum) * scaling).astype(jnp.bfloat16)
        outs[0, c] = attended
        outs[1, c] = matmul(score_half, key, ((1,), (0,))).astype(jnp.bfloat16)
        key_grad = matmul(score_half, query, ((0,), (0,)))
        value_grad = matmul(prob_half, grad, ((0,), (0,)))
        sums[first, 0] += key_grad[:key_len]
        sums[first, 1] += value_grad[:key_len]
        sums[second, 0] += key_grad[key_len:]
        sums[second, 1] += value_grad[key_len:]
        return 0

    lax.fori_loop(0, groups, one_group, 0, unroll=UNROLL)
    grads[...] = sums[...].astype(grads.dtype)


def attention(nbr, tokens, memory, head_width):
    _, groups, group_len, columns = tokens.shape
    entries, _, key_len, _ = memory.shape
    once = pl.Buffered(1) if entries > 64 else None

    def token_spec():
        return pl.BlockSpec((2, groups, group_len, head_width), lambda h, n: (0, 0, 0, h))

    def memory_spec():
        return pl.BlockSpec(
            (entries, 2, key_len, head_width), lambda h, n: (0, 0, 0, h), pipeline_mode=once
        )

    return pl.pallas_call(
        functools.partial(attention_kernel, 1.0 / math.sqrt(head_width)),
        out_shape=(
            jax.ShapeDtypeStruct(tokens.shape, jnp.bfloat16),
            jax.ShapeDtypeStruct(memory.shape, jnp.bfloat16),
        ),
        grid_spec=pltpu.PrefetchScalarGridSpec(
            num_scalar_prefetch=1,
            grid=(columns // head_width,),
            in_specs=[token_spec(), memory_spec()],
            out_specs=[token_spec(), memory_spec()],
            scratch_shapes=[pltpu.VMEM((entries, 2, key_len, head_width), jnp.float32)],
        ),
        compiler_params=pltpu.CompilerParams(vmem_limit_bytes=52 * 2**20),
    )(nbr, tokens, memory)


def per_device(queries, keys, values, grad_out, neighbour_owner, neighbour_row):
    pieces = lax.axis_size("seq")
    group_dev, _, feature_count = queries.shape
    shard_rows = keys.shape[0]
    columns = feature_count // pieces
    head_width = feature_count // HEADS
    start = lax.axis_index("seq") * columns
    nbr_all = (neighbour_owner * shard_rows + neighbour_row).astype(jnp.int32)
    nbr = lax.dynamic_slice_in_dim(nbr_all, lax.axis_index("mem") * group_dev, group_dev, 0)
    own = jnp.stack(
        [
            lax.dynamic_slice_in_dim(keys, start, columns, 2),
            lax.dynamic_slice_in_dim(values, start, columns, 2),
        ],
        axis=1,
    )
    memory = lax.all_gather(own, "mem", axis=0, tiled=True)
    tokens = lax.all_to_all(
        jnp.stack([queries, grad_out]), "seq", split_axis=3, concat_axis=2, tiled=True
    )
    outs, grads = attention(nbr, tokens, memory, head_width)
    grads = lax.psum_scatter(grads, "mem", scatter_dimension=0, tiled=True)
    outs = lax.all_to_all(outs, "seq", split_axis=2, concat_axis=3, tiled=True)
    grads = lax.all_to_all(grads, "seq", split_axis=2, concat_axis=3, tiled=True)
    return (outs[0], outs[1], grads[:, 0], grads[:, 1])


def solution(mesh):
    tokens, whole = P("mem", "seq", None), P("mem", None, None)
    return jax.shard_map(
        per_device,
        mesh=mesh,
        in_specs=(tokens, whole, whole, tokens, P(), P()),
        out_specs=(tokens,) * 4,
        check_vma=False,
    )
```
